1024 devices in a mesh: grp: 16 (over z, core), own: 64 (over x, y).
Axes of the slice: x: 8, y: 8, z: 8, core: 2. Of those that a mesh axis runs over, the one named last changes fastest.
Arguments:
- embeddings: bfloat16 [262144, 1024], P(('grp', 'own')), may hold values from -180 to 180
- coarse_id: int32 [262144], P(('grp', 'own')), may hold values from 0 to 511, as said below
- fine_count: int32 [64, 8], P('own'), may hold values from 1 to 128, 512 in all within a row
- fine: bfloat16 [32768, 1024], P('own'), may hold values from -6 to 6
Outputs:
- fine_new: bfloat16 [32768, 1024], P('own')
- coarse_new: bfloat16 [512, 1024], P('own', 'grp')
The draws below stay inside these ranges and needn't reach their ends.
Inputs may be any that keep to these rules, and one draw needn't show every extreme that they name: `coarse_id`: among the rows of one device, at most 8 name coarse clusters of one owner (o * 8 to (o + 1) * 8 - 1), and for some owner exactly 8 do. `fine_count`: each row sums to 512; some range holds exactly 128.
All inputs are finite; a program needn't handle non-finite values.
Results may differ from the reference program's by a relative error of at most 0.015.
Values may be sent and summed in bfloat16 or wider, within the bound.
A program may use at most 32 MiB of HBM per device.

```python
import math
import jax
import jax.numpy as jnp
import numpy as np
from jax import lax

D = 1024
F_OWN = 512
KC_OWN = 8
MAXF = 128
ROWS_DEV = 256
CAP = 8
GROUP_ROWS = 16384
TOKENS = 262144
KF = 32768
KC = 512
N_GRP = 16
N_OWN = 64


def draw_embeddings(key, part):
    key = jax.random.fold_in(key, 5)
    first = jax.random.fold_in(key, 0)
    return jnp.clip(jax.random.normal(first, (TOKENS, D), jnp.float32), -6.0, 6.0).astype(jnp.bfloat16)


def draw_coarse_id(key, part):
    key = jax.random.fold_in(key, 11)
    owners = KC // KC_OWN
    blocks = TOKENS // ROWS_DEV

    def one_block(block_key):
        first, second, third, fourth = jax.random.split(block_key, 4)
        hot = jax.random.randint(first, (), 0, owners)
        priority = jax.random.permutation(second, owners * CAP).astype(jnp.int32)
        slot = jnp.arange(owners * CAP, dtype=jnp.int32)
        priority = priority - (slot // CAP == hot).astype(jnp.int32) * (owners * CAP)
        chosen = jnp.argsort(priority, stable=True)[:ROWS_DEV].astype(jnp.int32)
        chosen = jax.random.permutation(third, chosen)
        local = jax.random.randint(fourth, (ROWS_DEV,), 0, KC_OWN)
        return chosen // CAP * KC_OWN + local
    keys = jax.random.split(key, blocks)
    return jax.vmap(one_block)(keys).reshape(TOKENS).astype(jnp.int32)


def level_of(key, shape, cuts, smallest, largest):
    gain, own = 1.0, jax.random.fold_in(key, 6)
    for dim, shards_of in cuts:
        steps = jnp.exp(jax.random.uniform(jax.random.fold_in(own, dim), (shards_of,), jnp.float32, smallest / len(cuts), largest / len(cuts)))
        gain = gain * jnp.repeat(steps, shape[dim] // shards_of).reshape([-1 if axis == dim else 1 for axis in range(len(shape))])
    return gain


def split_up(count, total, bound, lean):
    loads = [(1 << 20) // math.isqrt(grade ** lean) + 1 for grade in range(2, count + 1)]
    surplus, given = total - bound - (count - 1), [1] * (count - 1)
    while surplus > 0:
        free = [i for i in range(count - 1) if given[i] < bound]
        pool, budget = sum([loads[i] for i in free]), surplus
        for i in free:
            extra = min(bound - given[i], max(1, budget * loads[i] // pool), surplus)
            given[i] = given[i] + extra
            surplus = surplus - extra
    return np.array([bound] + given)


def uneven_parts(rng, number_of, total, reach, skew):
    if number_of == 2:
        one = jax.random.randint(rng, (), max(1, total - reach), min(reach, total - 1) + 1)
        return jnp.stack([one, total - one])
    tallies = jnp.asarray(split_up(number_of, total, reach, skew), jnp.int32)
    couples = (number_of - 1) // 2
    source_of, taker = tallies[1:1 + 2 * couples:2], tallies[2:2 + 2 * couples:2]
    slack = jnp.minimum(source_of - 1, reach - taker)
    shifted = jax.random.randint(jax.random.fold_in(rng, 1), (couples,), 0, 1 << 20) % (slack + 1)
    tallies = tallies.at[1:1 + 2 * couples:2].set(source_of - shifted).at[2:2 + 2 * couples:2].set(taker + shifted)
    return tallies[jax.random.permutation(jax.random.fold_in(rng, 2), number_of)]


def bell_draw(key, extent, scale, limit, pieces=(), held_as=jnp.bfloat16):
    result = jax.random.normal(key, extent, jnp.float32) * scale
    if len(pieces) > 0:
        result = level_of(key, extent, pieces, -0.22, 0.18) * result
    return jnp.clip(result, min=-limit, max=limit).astype(held_as)


def setup_inputs(seed: int = 0) -> dict:
    seeds = jax.random.split(jax.random.key(seed), 5)
    embeddings = draw_embeddings(jax.random.fold_in(seeds[4], 71), 0)
    coarse_id = draw_coarse_id(jax.random.fold_in(seeds[4], 71), 0)
    fine_count = jax.vmap(lambda own: uneven_parts(own, KC_OWN, F_OWN, MAXF, 2))(jax.random.split(seeds[2], N_OWN)).reshape((N_OWN, KC_OWN)).astype(jnp.int32)
    fine = bell_draw(seeds[3], (KF, D), 1.0, 6.0, ((0, 64),))
    return dict(embeddings=embeddings, coarse_id=coarse_id, fine_count=fine_count, fine=fine)


def fine_clusters(lengths, count):
    starts = jnp.cumsum(lengths) - lengths
    index = jnp.arange(count, dtype=jnp.int32)
    inside = (index[:, None] >= starts[None, :]).astype(jnp.int32)
    return (jnp.sum(inside, axis=1) - 1).astype(jnp.int32)


def respond(rows, label, shard, cluster):
    member = cluster[None, :] == label[:, None]
    squares = jnp.sum(jnp.square(shard.astype(jnp.float32)), axis=1)
    dots = lax.dot_general(rows, shard, (((1,), (1,)), ((), ())), preferred_element_type=jnp.float32)
    scores = (dots - 0.5 * squares[None, :]) * (rows.shape[1] ** -0.5)
    masked = jnp.where(member, scores, -1e30)
    top = jnp.max(masked, axis=1, keepdims=True)
    weights = jnp.where(member, jnp.exp(masked - top), 0.0)
    total = jnp.sum(weights, axis=1, keepdims=True)
    valid = (label >= 0).astype(jnp.float32)
    resp = (weights / (total + (1.0 - valid)[:, None])).astype(jnp.bfloat16)
    sums = lax.dot_general(resp, rows, (((0,), (0,)), ((), ())), preferred_element_type=jnp.float32)
    counts = jnp.sum(resp.astype(jnp.float32), axis=0)
    return sums, counts


def update(sums, counts, fine_cols, cluster):
    member = (cluster[None, :] == jnp.arange(KC_OWN, dtype=jnp.int32)[:, None]).astype(jnp.float32)
    numer = sums + fine_cols.astype(jnp.float32)
    weight = counts + 1.0
    fine_next = (numer / weight[:, None]).astype(jnp.bfloat16)
    coarse_num = jnp.dot(member, numer, precision=lax.Precision.HIGHEST)
    coarse_den = jnp.dot(member, weight, precision=lax.Precision.HIGHEST)
    return fine_next, (coarse_num / coarse_den[:, None]).astype(jnp.bfloat16)


def reference(embeddings, coarse_id, fine_count, fine):
    slots = N_OWN * CAP

    def per_owner(owner):
        shard = lax.dynamic_slice_in_dim(fine, owner * F_OWN, F_OWN, 0)
        lengths = lax.dynamic_index_in_dim(fine_count, owner, 0, keepdims=False)
        cluster = fine_clusters(lengths, F_OWN)

        def per_group(group, carry):
            acc_sums, acc_counts = carry
            rows = lax.dynamic_slice_in_dim(embeddings, group * GROUP_ROWS, GROUP_ROWS, 0)
            labels = lax.dynamic_slice_in_dim(coarse_id, group * GROUP_ROWS, GROUP_ROWS, 0)
            hit = labels // KC_OWN == owner
            (picked_at,) = jnp.nonzero(hit, size=slots, fill_value=0)
            picked_at = picked_at.astype(jnp.int32)
            taken = jnp.arange(slots, dtype=jnp.int32) < jnp.sum(hit.astype(jnp.int32))
            label = jnp.where(taken, labels[picked_at] - owner * KC_OWN, -1).astype(jnp.int32)
            sums, counts = respond(rows[picked_at], label, shard, cluster)
            rounded = lax.optimization_barrier(sums.astype(jnp.bfloat16)).astype(jnp.float32)
            return acc_sums + rounded, acc_counts + counts

        start = (jnp.zeros((F_OWN, D), jnp.float32), jnp.zeros((F_OWN,), jnp.float32))
        acc_sums, acc_counts = lax.fori_loop(0, N_GRP, per_group, start)
        return update(acc_sums, acc_counts, shard, cluster)

    fines, coarses = lax.map(per_owner, jnp.arange(N_OWN, dtype=jnp.int32))
    return fines.reshape(KF, D), coarses.reshape(KC, D)
```

```python
import functools

import jax
import jax.numpy as jnp
from jax import lax
from jax.experimental import pallas as pl
from jax.experimental.pallas import tpu as pltpu
from jax.sharding import PartitionSpec as P

KC_OWN = 8
CAP = 8
LANES = 128


def torus(owners):
    fast = 1
    while fast * fast < owners:
        fast *= 2
    return owners // fast, fast


def iota(shape, dim):
    return lax.broadcasted_iota(jnp.int32, shape, dim)


def to_column(row):
    n = row.shape[1]
    return jnp.sum(jnp.where(iota((n, n), 0) == iota((n, n), 1), row, 0.0), axis=1, keepdims=True)


def kernel(
    owners, groups,
    emb, cid, fine_count, fine,
    fine_new, coarse_new,
    out_rows, in_rows, out_tags, in_tags, rows, resp, own_part, sib_out, sib_in,
    right_out, right_in, left_out, left_in, cnt_out, cnt_in, num_out, num_in, table,
    send_rows, recv_rows, send_tags, recv_tags, send_sib, recv_sib,
    send_right, recv_right, send_left, recv_left, send_cnt, recv_cnt, send_num, recv_num,
    send_gr, recv_gr, send_gl, recv_gl, send_gs, recv_gs, send_home,
):
    nx, ny = torus(owners)
    nz = groups // 2
    rows_dev, width = emb.shape
    half = width // 2
    f_own = fine.shape[0]
    f_half = f_own // 2
    chunk = min(16, owners)
    chunks = owners // chunk
    slots = chunk * CAP
    right_steps, left_steps = nz // 2, nz // 2 - 1
    bf16, f32 = jnp.bfloat16, jnp.float32

    own = lax.axis_index("own")
    grp = lax.axis_index("grp")
    mx, my = own // ny, own % ny
    z, core = grp // 2, grp % 2
    sibling = {"grp": z * 2 + 1 - core}
    right = {"grp": lax.rem(z + 1, nz) * 2 + core}
    left = {"grp": lax.rem(z + nz - 1, nz) * 2 + core}

    def peer(i):
        kx, b = lax.rem(i, nx), i // nx
        ky = lax.rem(3 * kx + b, ny)
        return {"own": lax.rem(mx + kx, nx) * ny + lax.rem(my + ky, ny)}

    def mate(i):
        return {"grp": lax.rem(grp + i, groups)}

    def remote(src, dst, send, recv, device):
        return pltpu.make_async_remote_copy(
            src_ref=src, dst_ref=dst, send_sem=send, recv_sem=recv,
            device_id=device, device_id_type=pl.DeviceIdType.MESH,
        )

    def take(ref, sem):
        pltpu.make_async_copy(ref, ref, sem).wait()

    barrier = pltpu.get_barrier_semaphore()

    @pl.loop(1, owners)
    def _(i):
        pl.semaphore_signal(barrier, inc=1, device_id=peer(i), device_id_type=pl.DeviceIdType.MESH)

    @pl.loop(1, groups)
    def _(i):
        pl.semaphore_signal(barrier, inc=1, device_id=mate(i), device_id_type=pl.DeviceIdType.MESH)

    ids = cid[...]
    owner = lax.shift_right_logical(ids, 3)
    kx = (lax.shift_right_logical(owner, ny.bit_length() - 1) - mx) & (nx - 1)
    ky = ((owner & (ny - 1)) - my) & (ny - 1)
    block = ((ky - 3 * kx) & (ny - 1)) * nx + kx
    owner_row = owner.astype(f32)
    owner_col = to_column(owner_row)
    local_col = to_column((ids & (KC_OWN - 1)).astype(f32))
    square = (rows_dev, rows_dev)
    same = owner_col == owner_row
    place_row = jnp.sum(jnp.where(same & (iota(square, 0) < iota(square, 1)), 1.0, 0.0), axis=0, keepdims=True)
    place_col = jnp.sum(jnp.where(same & (iota(square, 1) < iota(square, 0)), 1.0, 0.0), axis=1, keepdims=True)
    target = block * (2 * CAP) + place_row.astype(jnp.int32)

    pick = (iota((owners, rows_dev), 0) == block).astype(bf16)
    lane = (iota((rows_dev, LANES), 1) & (CAP - 1)).astype(f32)
    spread = jnp.where(place_col == lane, local_col + 1.0, 0.0).astype(bf16)
    tags = jnp.dot(pick, spread, preferred_element_type=f32)
    out_tags[...] = tags.reshape(owners, 1, LANES)
    in_tags[0] = out_tags[0]

    def build(c):
        tall = 2 * CAP * chunk
        at = iota((tall, rows_dev), 0) + c * tall
        low = (at == target).astype(bf16)
        high = (at == target + CAP).astype(bf16)
        made = jnp.dot(low, emb[:, :half], preferred_element_type=f32)
        made += jnp.dot(high, emb[:, half:], preferred_element_type=f32)
        out_rows[pl.ds(c * chunk, chunk)] = made.astype(bf16).reshape(chunk, 2 * CAP, half)

    build(0)
    pl.semaphore_wait(barrier, owners + groups - 2)
    for c in range(chunks):
        if c > 0:
            build(c)

        @pl.loop(max(1, c * chunk), (c + 1) * chunk)
        def _(i):
            remote(out_tags.at[i], in_tags.at[i], send_tags.at[0], recv_tags.at[c], peer(i)).start()
            remote(out_rows.at[i], in_rows.at[i], send_rows.at[0], recv_rows.at[c], peer(i)).start()

    in_rows[0] = out_rows[0]

    fine_rows = fine[...].astype(f32)
    squares = jnp.sum(fine_rows * fine_rows, axis=1, keepdims=True)
    index_col, index_row = iota((f_own, 1), 0), iota((1, f_own), 1)
    cluster_col = jnp.zeros((f_own, 1), jnp.int32)
    cluster_row = jnp.zeros((1, f_own), jnp.int32)
    start = jnp.int32(0)
    for k in range(KC_OWN - 1):
        start = start + fine_count[0, k]
        cluster_col += (index_col >= start).astype(jnp.int32)
        cluster_row += (index_row >= start).astype(jnp.int32)
    table[...] = jnp.broadcast_to(squares * 0.5, table.shape)
    cluster_of = cluster_col.astype(f32)
    member_of = (cluster_row == iota((KC_OWN, f_own), 0)).astype(f32)

    for c in range(chunks):
        lo = max(1, c * chunk)
        part = pl.ds(lo, (c + 1) * chunk - lo)
        take(in_tags.at[part], recv_tags.at[c])
        take(in_rows.at[part], recv_rows.at[c])
        here = pl.ds(c * chunk, chunk)
        tag = in_tags[here].reshape(chunk, LANES)[:, :slots]
        tag = jnp.where(iota((chunk, slots), 1) // CAP == iota((chunk, slots), 0), tag, 0.0)
        label = jnp.sum(tag, axis=0, keepdims=True) - 1.0
        wide = in_rows[here].astype(f32).reshape(chunk, 2, CAP, half)
        low = wide[:, 0].reshape(slots, half).astype(bf16)
        high = wide[:, 1].reshape(slots, half).astype(bf16)
        at = pl.ds(c * slots, slots)
        for b in range(nz // 2):
            rows[b, at, :] = low[:, b * LANES:(b + 1) * LANES]
            rows[nz // 2 + b, at, :] = high[:, b * LANES:(b + 1) * LANES]
        flip = (((1,), (1,)), ((), ()))
        dots = lax.dot_general(fine[:, :half], low, flip, preferred_element_type=f32)
        dots += lax.dot_general(fine[:, half:], high, flip, preferred_element_type=f32)
        member = cluster_of == label
        scores = (dots - table[:, :slots]) * (width ** -0.5)
        masked = jnp.where(member, scores, -1e30)
        top = jnp.max(masked, axis=0, keepdims=True)
        weights = jnp.where(member, jnp.exp(masked - top), 0.0)
        total = jnp.sum(weights, axis=0, keepdims=True)
        empty = (label < 0.0).astype(f32)
        resp[:, at] = (weights / (total + empty)).astype(bf16)

    mine, other = pl.ds(core * f_half, f_half), pl.ds((1 - core) * f_half, f_half)
    order = []
    for t in range(right_steps):
        order.append(right_steps - t)
        if t < left_steps:
            order.append(nz - left_steps + t)
    order.append(0)
    for off in order:
        b = lax.rem(z + off, nz)
        sib_out[b] = jnp.dot(resp[other, :], rows[b], preferred_element_type=f32).astype(bf16)
        remote(sib_out.at[b], sib_in.at[b], send_sib.at[b], recv_sib.at[b], sibling).start()
        own_part[b] = jnp.dot(resp[mine, :], rows[b], preferred_element_type=f32)

    ones = jnp.ones((8, resp.shape[1]), bf16)
    counts = lax.dot_general(ones, resp[...], (((1,), (1,)), ((), ())), preferred_element_type=f32)
    cnt_out[...] = counts[0:1, :]
    cnt_in[0] = counts[0:1, :]

    @pl.loop(1, groups)
    def _(i):
        remote(cnt_out, cnt_in.at[i], send_cnt.at[0], recv_cnt.at[0], mate(i)).start()

    def chip(b):
        take(sib_in.at[b], recv_sib.at[b])
        return own_part[b] + sib_in[b].astype(f32)

    for t in range(right_steps):
        total = chip(lax.rem(z + right_steps - t, nz))
        if t > 0:
            take(right_in.at[t - 1], recv_right.at[t - 1])
            total += right_in[t - 1].astype(f32)
        right_out[t] = total.astype(bf16)
        remote(right_out.at[t], right_in.at[t], send_right.at[t], recv_right.at[t], right).start()
        if t < left_steps:
            total = chip(lax.rem(z + nz - left_steps + t, nz))
            if t > 0:
                take(left_in.at[t - 1], recv_left.at[t - 1])
                total += left_in[t - 1].astype(f32)
            left_out[t] = total.astype(bf16)
            remote(left_out.at[t], left_in.at[t], send_left.at[t], recv_left.at[t], left).start()

    take(cnt_in.at[pl.ds(1, groups - 1)], recv_cnt.at[0])
    count = jnp.sum(cnt_in[...], axis=0)
    weight = count + 1.0
    count_half = jnp.where(core == 0, weight[:, :f_half], weight[:, f_half:])
    weight_col = to_column(count_half)
    den = jnp.sum(member_of * weight, axis=1, keepdims=True)
    member_half = jnp.where(core == 0, member_of[:, :f_half], member_of[:, f_half:])

    columns = pl.ds(pl.multiple_of(z * LANES, LANES), LANES)
    numer = chip(z) + fine[mine, columns].astype(f32)
    if left_steps > 0:
        take(left_in.at[left_steps - 1], recv_left.at[left_steps - 1])
        numer += left_in[left_steps - 1].astype(f32)
    take(right_in.at[right_steps - 1], recv_right.at[right_steps - 1])
    numer += right_in[right_steps - 1].astype(f32)
    fine_new[mine, columns] = (numer / weight_col).astype(bf16)

    def spot(b):
        return fine_new.at[mine, pl.ds(pl.multiple_of(b * LANES, LANES), LANES)]

    def to_sibling(b):
        remote(spot(b), spot(b), send_gs.at[0], recv_gs.at[0], sibling).start()

    def to_right(t):
        b = lax.rem(z + nz - t, nz)
        remote(spot(b), spot(b), send_gr.at[t], recv_gr.at[t], right).start()

    def to_left(t):
        b = lax.rem(z + t, nz)
        remote(spot(b), spot(b), send_gl.at[t], recv_gl.at[t], left).start()

    to_right(0)
    if left_steps > 0:
        to_left(0)
    to_sibling(z)

    num = lax.dot_general(
        member_half, numer, (((1,), (0,)), ((), ())),
        preferred_element_type=f32, precision=lax.Precision.HIGHEST,
    )
    num_out[...] = num
    remote(num_out, num_in, send_num.at[0], recv_num.at[0], sibling).start()

    for t in range(right_steps):
        b = lax.rem(z + nz - 1 - t, nz)
        take(spot(b), recv_gr.at[t])
        if t + 1 < right_steps:
            to_right(t + 1)
        to_sibling(b)
        if t < left_steps:
            b = lax.rem(z + 1 + t, nz)
            take(spot(b), recv_gl.at[t])
            if t + 1 < left_steps:
                to_left(t + 1)
            to_sibling(b)

    take(num_in, recv_num.at[0])
    coarse = (num + num_in[...]) / den
    coarse = jnp.where(core == 0, coarse[:, :LANES // 2], coarse[:, LANES // 2:])
    coarse_new[...] = coarse.astype(bf16)

    take(out_rows.at[pl.ds(1, owners - 1)], send_rows.at[0])
    take(out_tags.at[pl.ds(1, owners - 1)], send_tags.at[0])
    take(cnt_in.at[pl.ds(1, groups - 1)], send_cnt.at[0])
    take(num_out, send_num.at[0])
    for b in range(nz):
        take(sib_out.at[b], send_sib.at[b])
    for t in range(right_steps):
        take(right_out.at[t], send_right.at[t])
        take(spot(0), send_gr.at[t])
    for t in range(left_steps):
        take(left_out.at[t], send_left.at[t])
        take(spot(0), send_gl.at[t])
    take(fine_new.at[mine, :], send_gs.at[0])
    take(fine_new.at[other, :], recv_gs.at[0])


def per_device(owners, groups, embeddings, coarse_id, fine_count, fine):
    rows_dev, width = embeddings.shape
    f_own = fine.shape[0]
    nz = groups // 2
    assert width == nz * LANES
    right_steps, left_steps = nz // 2, nz // 2 - 1
    chunk = min(16, owners)
    chunks = owners // chunk
    slots = owners * CAP
    bf16, f32 = jnp.bfloat16, jnp.float32
    vmem, dma = pltpu.VMEM, pltpu.SemaphoreType.DMA
    in_vmem = pl.BlockSpec(memory_space=pltpu.VMEM)
    piece = (f_own // 2, LANES)
    return pl.pallas_call(
        functools.partial(kernel, owners, groups),
        out_shape=(
            jax.ShapeDtypeStruct((f_own, width), bf16),
            jax.ShapeDtypeStruct((KC_OWN, width // groups), bf16),
        ),
        in_specs=[in_vmem, in_vmem, pl.BlockSpec(memory_space=pltpu.SMEM), in_vmem],
        out_specs=(in_vmem, in_vmem),
        scratch_shapes=[
            vmem((owners, 2 * CAP, width // 2), bf16),
            vmem((owners, 2 * CAP, width // 2), bf16),
            vmem((owners, 1, LANES), f32),
            vmem((owners, 1, LANES), f32),
            vmem((nz, slots, LANES), bf16),
            vmem((f_own, slots), bf16),
            vmem((nz,) + piece, f32),
            vmem((nz,) + piece, bf16),
            vmem((nz,) + piece, bf16),
            vmem((right_steps,) + piece, bf16),
            vmem((right_steps,) + piece, bf16),
            vmem((max(1, left_steps),) + piece, bf16),
            vmem((max(1, left_steps),) + piece, bf16),
            vmem((1, f_own), f32),
            vmem((groups, 1, f_own), f32),
            vmem((KC_OWN, LANES), f32),
            vmem((KC_OWN, LANES), f32),
            vmem((f_own, LANES), f32),
            dma((1,)), dma((chunks,)), dma((1,)), dma((chunks,)), dma((nz,)), dma((nz,)),
            dma((right_steps,)), dma((right_steps,)), dma((max(1, left_steps),)), dma((max(1, left_steps),)),
            dma((1,)), dma((1,)), dma((1,)), dma((1,)),
            dma((right_steps,)), dma((right_steps,)), dma((max(1, left_steps),)), dma((max(1, left_steps),)),
            dma((1,)), dma((1,)), dma((1,)),
        ],
        compiler_params=pltpu.CompilerParams(
            collective_id=0, has_side_effects=True, vmem_limit_bytes=40 * 1024 * 1024
        ),
    )(embeddings, coarse_id.reshape(1, rows_dev), fine_count, fine)


def solution(mesh):
    return jax.shard_map(
        functools.partial(per_device, mesh.shape["own"], mesh.shape["grp"]),
        mesh=mesh,
        in_specs=(P(("grp", "own"), None), P(("grp", "own")), P("own", None), P("own", None)),
        out_specs=(P("own", None), P("own", "grp")),
        check_vma=False,
    )
```

```python
import functools

import jax
import jax.numpy as jnp
from jax import lax
from jax.experimental import pallas as pl
from jax.experimental.pallas import tpu as pltpu
from jax.sharding import PartitionSpec as P

KC_OWN = 8
CAP = 8
LANES = 128


def torus(owners):
    fast = 1
    while fast * fast < owners:
        fast *= 2
    return owners // fast, fast


def turned(a, b, r):
    return ((a, b), (-b, a), (-a, -b), (b, -a))[r]


def far_first(nx, ny):
    if (nx, ny) != (8, 8):
        return [(i % nx, i // nx) for i in range(nx * ny)]
    order = []
    for g in range(16):
        a, b = 4 - g // 4, 3 - g % 4
        if (a, b) == (4, 0):
            order += [(4, 0), (0, 4), (0, 0), (4, 4)]
        else:
            order += [turned(a, b, r) for r in range(4)]
    return [(a % nx, b % ny) for a, b in order]


def iota(shape, dim):
    return lax.broadcasted_iota(jnp.int32, shape, dim)


def to_column(row):
    n = row.shape[1]
    return jnp.sum(jnp.where(iota((n, n), 0) == iota((n, n), 1), row, 0.0), axis=1, keepdims=True)


def kernel(
    owners, groups,
    emb_hbm, cid_hbm, count_hbm, fine_hbm,
    fine_new, coarse_new,
    emb, cid, fine_count, fine,
    out_rows, in_rows, out_tags, in_tags, rows, resp, own_part, sib_out, sib_in,
    out4, in4, out3, in3, out2, in2, out1, in1, cnt_out, cnt_in, num_out, num_in, table, ring_new,
    load, send_rows, recv_rows, send_tags, recv_tags, send_sib, recv_sib,
    send_sum, recv_sum, send_cnt, recv_cnt, send_num, recv_num, send_ring, recv_ring, send_gs, recv_gs, keep,
):
    nx, ny = torus(owners)
    nz = groups // 2
    rows_dev, width = emb.shape
    half = width // 2
    f_own = fine.shape[0]
    f_half = f_own // 2
    f_quarter = f_own // 4
    chunk = min(16, owners)
    chunks = owners // chunk
    slots = chunk * CAP
    bf16, f32 = jnp.bfloat16, jnp.float32

    own = lax.axis_index("own")
    grp = lax.axis_index("grp")
    mx, my = own // ny, own % ny
    z, core = grp // 2, grp % 2
    sibling = {"grp": z * 2 + 1 - core}

    order = far_first(nx, ny)
    here = order.index((0, 0))

    def peer(kx, ky):
        return {"own": lax.rem(mx + kx + nx, nx) * ny + lax.rem(my + ky + ny, ny)}

    def for_peers(lo, hi, act):
        if (nx, ny) != (8, 8):
            for i in range(lo, hi):
                if i != here:
                    act(i, peer(*order[i]))
            return

        def four(g):
            a, b = 4 - g // 4, 3 - lax.rem(g, 4)
            for r in range(4):
                act(g * 4 + r, peer(*turned(a, b, r)))

        first, last = lo // 4, hi // 4
        if first <= 3 < last:
            pl.loop(first, 3)(four)
            for i in (12, 13, 15):
                act(i, peer(*order[i]))
            first = 4
        pl.loop(first, last)(four)

    def along(k):
        return lax.rem(z + k + nz, nz)

    def at_z(k):
        return {"grp": along(k) * 2 + core}

    def mate(i):
        return {"grp": lax.rem(grp + i, groups)}

    def remote(src, dst, send, recv, device):
        return pltpu.make_async_remote_copy(
            src_ref=src, dst_ref=dst, send_sem=send, recv_sem=recv,
            device_id=device, device_id_type=pl.DeviceIdType.MESH,
        )

    def take(ref, sem):
        pltpu.make_async_copy(ref, ref, sem).wait()

    loads = [
        pltpu.make_async_copy(src, dst, load.at[n])
        for n, (src, dst) in enumerate(
            ((cid_hbm, cid), (emb_hbm, emb), (count_hbm, fine_count), (fine_hbm, fine))
        )
    ]
    for copy in loads:
        copy.start()

    barrier = pltpu.get_barrier_semaphore()

    def greet(i, device):
        pl.semaphore_signal(barrier, inc=1, device_id=device, device_id_type=pl.DeviceIdType.MESH)

    for_peers(0, owners, greet)

    @pl.loop(1, groups)
    def _(i):
        greet(i, mate(i))

    loads[0].wait()
    ids = cid[...]
    owner = lax.shift_right_logical(ids, 3)
    kx = (lax.shift_right_logical(owner, ny.bit_length() - 1) - mx) & (nx - 1)
    ky = ((owner & (ny - 1)) - my) & (ny - 1)
    away = kx * ny + ky
    block = jnp.zeros_like(away)
    for i, (a, b) in enumerate(order):
        block = jnp.where(away == a * ny + b, i, block)
    owner_row = owner.astype(f32)
    owner_col = to_column(owner_row)
    local_col = to_column((ids & (KC_OWN - 1)).astype(f32))
    square = (rows_dev, rows_dev)
    same = owner_col == owner_row
    place_row = jnp.sum(jnp.where(same & (iota(square, 0) < iota(square, 1)), 1.0, 0.0), axis=0, keepdims=True)
    place_col = jnp.sum(jnp.where(same & (iota(square, 1) < iota(square, 0)), 1.0, 0.0), axis=1, keepdims=True)
    target = block * (2 * CAP) + place_row.astype(jnp.int32)

    pick = (iota((owners, rows_dev), 0) == block).astype(bf16)
    lane = (iota((rows_dev, LANES), 1) & (CAP - 1)).astype(f32)
    spread = jnp.where(place_col == lane, local_col + 1.0, 0.0).astype(bf16)
    tags = jnp.dot(pick, spread, preferred_element_type=f32)
    out_tags[...] = tags.reshape(owners, 1, LANES)
    in_tags[here] = out_tags[here]

    loads[1].wait()
    for c in range(chunks):
        tall = 2 * CAP * chunk
        at = iota((tall, rows_dev), 0) + c * tall
        low = (at == target).astype(bf16)
        high = (at == target + CAP).astype(bf16)
        made = jnp.dot(low, emb[:, :half], preferred_element_type=f32)
        made += jnp.dot(high, emb[:, half:], preferred_element_type=f32)
        out_rows[pl.ds(c * chunk, chunk)] = made.astype(bf16).reshape(chunk, 2 * CAP, half)

    pl.semaphore_wait(barrier, owners + groups - 2)
    for c in range(chunks):

        def send(i, device):
            remote(out_tags.at[i], in_tags.at[i], send_tags.at[0], recv_tags.at[c], device).start()
            remote(out_rows.at[i], in_rows.at[i], send_rows.at[0], recv_rows.at[c], device).start()

        for_peers(c * chunk, (c + 1) * chunk, send)

    in_rows[here] = out_rows[here]

    loads[2].wait()
    loads[3].wait()
    fine_rows = fine[...].astype(f32)
    squares = jnp.sum(fine_rows * fine_rows, axis=1, keepdims=True)
    index_col, index_row = iota((f_own, 1), 0), iota((1, f_own), 1)
    cluster_col = jnp.zeros((f_own, 1), f32)
    cluster_row = jnp.zeros((1, f_own), f32)
    start = jnp.zeros((1, 1), jnp.int32)
    for k in range(KC_OWN - 1):
        start = start + fine_count[:, k:k + 1]
        cluster_col += (index_col >= start).astype(f32)
        cluster_row += (index_row >= start).astype(f32)
    table[...] = jnp.broadcast_to(squares * 0.5, table.shape)
    member_of = (cluster_row == iota((KC_OWN, f_own), 0).astype(f32)).astype(f32)

    for c in range(chunks):
        gone = chunk - (1 if c == here // chunk else 0)
        if gone > 0:
            take(in_tags.at[pl.ds(c * chunk, gone)], recv_tags.at[c])
            take(in_rows.at[pl.ds(c * chunk, gone)], recv_rows.at[c])
        these = pl.ds(c * chunk, chunk)
        tag = in_tags[these].reshape(chunk, LANES)[:, :slots]
        tag = jnp.where(iota((chunk, slots), 1) // CAP == iota((chunk, slots), 0), tag, 0.0)
        label = jnp.sum(tag, axis=0, keepdims=True) - 1.0
        wide = in_rows[these].astype(f32).reshape(chunk, 2, CAP, half)
        low = wide[:, 0].reshape(slots, half).astype(bf16)
        high = wide[:, 1].reshape(slots, half).astype(bf16)
        at = pl.ds(c * slots, slots)
        for b in range(nz // 2):
            rows[b, at, :] = low[:, b * LANES:(b + 1) * LANES]
            rows[nz // 2 + b, at, :] = high[:, b * LANES:(b + 1) * LANES]
        flip = (((1,), (1,)), ((), ()))
        dots = lax.dot_general(fine[:, :half], low, flip, preferred_element_type=f32)
        dots += lax.dot_general(fine[:, half:], high, flip, preferred_element_type=f32)
        member = cluster_col == label
        scores = (dots - table[:, :slots]) * (width ** -0.5)
        masked = jnp.where(member, scores, -1e30)
        top = jnp.max(masked, axis=0, keepdims=True)
        weights = jnp.where(member, jnp.exp(masked - top), 0.0)
        total = jnp.sum(weights, axis=0, keepdims=True)
        empty = (label < 0.0).astype(f32)
        resp[:, at] = (weights / (total + empty)).astype(bf16)

    mine, other = pl.ds(core * f_half, f_half), pl.ds((1 - core) * f_half, f_half)

    def weigh(off):
        b = along(off)
        sib_out[b] = jnp.dot(resp[other, :], rows[b], preferred_element_type=f32).astype(bf16)
        remote(sib_out.at[b], sib_in.at[b], send_sib.at[b], recv_sib.at[b], sibling).start()
        own_part[b] = jnp.dot(resp[mine, :], rows[b], preferred_element_type=f32)

    def count_up():
        ones = jnp.ones((8, resp.shape[1]), bf16)
        counts = lax.dot_general(ones, resp[...], (((1,), (1,)), ((), ())), preferred_element_type=f32)
        cnt_out[...] = counts[0:1, :]
        cnt_in[0] = counts[0:1, :]

        @pl.loop(1, groups)
        def _(i):
            remote(cnt_out, cnt_in.at[i], send_cnt.at[0], recv_cnt.at[0], mate(i)).start()

    def chip(off, q):
        piece = pl.ds(q * f_quarter, f_quarter)
        b = along(off)
        return own_part[b, piece, :] + sib_in[b, piece, :].astype(f32)

    def both(off):
        b = along(off)
        take(sib_in.at[b], recv_sib.at[b])
        return own_part[b] + sib_in[b].astype(f32)

    sent = []

    def give(n, src, dst, k):
        remote(src, dst, send_sum.at[n], recv_sum.at[n], at_z(k)).start()
        sent.append((src, send_sum.at[n]))

    def got(n, ref):
        take(ref, recv_sum.at[n])
        return ref[...].astype(f32)

    for off in (4, 3, -3):
        weigh(off)
    total = both(4).astype(bf16)
    for q, k in ((0, -2), (1, 2)):
        out4[q] = total[q * f_quarter:(q + 1) * f_quarter]
        give(q, out4.at[q], in4.at[q], k)
    for n, off, k in ((0, -3, -1), (1, 3, 1)):
        out3[n] = both(off).astype(bf16)
        give(2 + n, out3.at[n], in3.at[n], k)
    for off in (2, -2):
        weigh(off)
    count_up()
    for off in (1, -1):
        weigh(off)
    for n, off in ((0, -1), (1, 1)):
        out1[n] = both(off).astype(bf16)
        give(4 + n, out1.at[n], in1.at[n], off)
    weigh(0)
    for off in (-2, 2, 0):
        take(sib_in.at[along(off)], recv_sib.at[along(off)])
    for n, off in ((0, -2), (1, 2)):
        take(in3.at[n], recv_sum.at[2 + n])
    for q in range(2):
        for n, off in ((1, 2), (0, -2)) if q == 0 else ((0, -2), (1, 2)):
            total = chip(off, q) + in3[n, pl.ds(q * f_quarter, f_quarter), :].astype(f32)
            if n == q:
                total += got(q, in4.at[q])
            out2[n, q] = total.astype(bf16)
            give(6 + 2 * n + q, out2.at[n, q], in2.at[n, q], off)

    take(cnt_in.at[pl.ds(1, groups - 1)], recv_cnt.at[0])
    weight = jnp.sum(cnt_in[...], axis=0) + 1.0
    weight_col = to_column(jnp.where(core == 0, weight[:, :f_half], weight[:, f_half:]))

    ring = []

    def part_of(off, q):
        return ring_new.at[along(off), pl.ds(q * f_quarter, f_quarter), :]

    def spread_to(n, off, q, k):
        piece = part_of(off, q)
        remote(piece, piece, send_ring.at[n], recv_ring.at[n], at_z(k)).start()
        ring.append((piece, send_ring.at[n]))

    def arrived(n, off, q):
        take(part_of(off, q), recv_ring.at[n])

    def hand_over(off):
        b = along(off)
        place = fine_new.at[mine, pl.ds(pl.multiple_of(b * LANES, LANES), LANES)]
        remote(ring_new.at[b], place, send_gs.at[0], recv_gs.at[0], sibling).start()
        pltpu.make_async_copy(ring_new.at[b], place, keep.at[0]).start()

    columns = pl.ds(pl.multiple_of(z * LANES, LANES), LANES)
    numers = []
    for n in range(2):
        take(in1.at[n], recv_sum.at[4 + n])
    for q in range(2):
        piece = pl.ds(q * f_quarter, f_quarter)
        old = fine[pl.ds(pl.multiple_of(core * f_half + q * f_quarter, f_quarter), f_quarter), columns]
        numer = chip(0, q) + old.astype(f32)
        numer += in1[0, piece, :].astype(f32) + in1[1, piece, :].astype(f32)
        numer += got(6 + q, in2.at[0, q]) + got(8 + q, in2.at[1, q])
        numers.append(numer)
        ring_new[z, piece, :] = (numer / weight_col[q * f_quarter:(q + 1) * f_quarter]).astype(bf16)
        spread_to(q, 0, q, 2)
        spread_to(2 + q, 0, q, -2)
    for q in range(2):
        spread_to(4 + q, 0, q, 1)
        spread_to(6 + q, 0, q, -1)
    hand_over(0)

    member_half = jnp.where(core == 0, member_of[:, :f_half], member_of[:, f_half:])
    num = sum(
        lax.dot_general(
            member_half[:, q * f_quarter:(q + 1) * f_quarter], numers[q], (((1,), (0,)), ((), ())),
            preferred_element_type=f32, precision=lax.Precision.HIGHEST,
        )
        for q in range(2)
    )
    num_out[...] = num
    remote(num_out, num_in, send_num.at[0], recv_num.at[0], sibling).start()
    den = jnp.sum(member_of * weight, axis=1, keepdims=True)

    arrived(0, -2, 0)
    spread_to(12, -2, 0, 2)
    spread_to(8, -2, 0, 1)
    arrived(2, 2, 0)
    spread_to(10, 2, 0, -1)
    arrived(3, 2, 1)
    spread_to(13, 2, 1, -2)
    spread_to(11, 2, 1, -1)
    arrived(1, -2, 1)
    spread_to(9, -2, 1, 1)
    hand_over(-2)
    hand_over(2)
    for n, off in ((4, -1), (6, 1)):
        arrived(n, off, 0)
        arrived(n + 1, off, 1)
        hand_over(off)

    take(num_in, recv_num.at[0])
    coarse = (num + num_in[...]) / den
    coarse = jnp.where(core == 0, coarse[:, :LANES // 2], coarse[:, LANES // 2:])
    coarse_new[...] = coarse.astype(bf16)

    for n, off in ((8, -3), (10, 3), (12, 4)):
        arrived(n, off, 0)
        arrived(n + 1, off, 1)
        hand_over(off)

    if owners > 1:
        take(out_rows.at[pl.ds(1, owners - 1)], send_rows.at[0])
        take(out_tags.at[pl.ds(1, owners - 1)], send_tags.at[0])
    take(cnt_in.at[pl.ds(1, groups - 1)], send_cnt.at[0])
    take(num_out, send_num.at[0])
    for b in range(nz):
        take(sib_out.at[b], send_sib.at[b])
    for ref, sem in sent + ring:
        take(ref, sem)
    take(ring_new, send_gs.at[0])
    take(ring_new, keep.at[0])
    take(fine_new.at[other, :], recv_gs.at[0])


def per_device(owners, groups, embeddings, coarse_id, fine_count, fine):
    rows_dev, width = embeddings.shape
    f_own = fine.shape[0]
    nz = groups // 2
    assert nz == 8
    chunks = max(1, owners // 16)
    slots = owners * CAP
    bf16, f32 = jnp.bfloat16, jnp.float32
    vmem, dma = pltpu.VMEM, pltpu.SemaphoreType.DMA
    anywhere = pl.BlockSpec(memory_space=pl.ANY)
    tile = (f_own // 2, LANES)
    piece = (f_own // 4, LANES)
    return pl.pallas_call(
        functools.partial(kernel, owners, groups),
        out_shape=(
            jax.ShapeDtypeStruct((f_own, width), bf16),
            jax.ShapeDtypeStruct((KC_OWN, width // groups), bf16),
        ),
        in_specs=[anywhere] * 4,
        out_specs=(anywhere, pl.BlockSpec(memory_space=pltpu.VMEM)),
        scratch_shapes=[
            vmem((rows_dev, width), bf16),
            vmem((1, rows_dev), jnp.int32),
            vmem((1, KC_OWN), jnp.int32),
            vmem((f_own, width), bf16),
            vmem((owners, 2 * CAP, width // 2), bf16),
            vmem((owners, 2 * CAP, width // 2), bf16),
            vmem((owners, 1, LANES), f32),
            vmem((owners, 1, LANES), f32),
            vmem((nz, slots, LANES), bf16),
            vmem((f_own, slots), bf16),
            vmem((nz,) + tile, f32),
            vmem((nz,) + tile, bf16),
            vmem((nz,) + tile, bf16),
            vmem((2,) + piece, bf16),
            vmem((2,) + piece, bf16),
            vmem((2,) + tile, bf16),
            vmem((2,) + tile, bf16),
            vmem((2, 2) + piece, bf16),
            vmem((2, 2) + piece, bf16),
            vmem((2,) + tile, bf16),
            vmem((2,) + tile, bf16),
            vmem((1, f_own), f32),
            vmem((groups, 1, f_own), f32),
            vmem((KC_OWN, LANES), f32),
            vmem((KC_OWN, LANES), f32),
            vmem((f_own, LANES), f32),
            vmem((nz,) + tile, bf16),
            dma((4,)),
            dma((1,)), dma((chunks,)), dma((1,)), dma((chunks,)), dma((nz,)), dma((nz,)),
            dma((10,)), dma((10,)), dma((1,)), dma((1,)), dma((1,)), dma((1,)),
            dma((14,)), dma((14,)), dma((1,)), dma((1,)), dma((1,)),
        ],
        compiler_params=pltpu.CompilerParams(
            collective_id=0, has_side_effects=True, vmem_limit_bytes=56 * 1024 * 1024
        ),
    )(embeddings, coarse_id.reshape(1, rows_dev), fine_count, fine)


def solution(mesh):
    return jax.shard_map(
        functools.partial(per_device, mesh.shape["own"], mesh.shape["grp"]),
        mesh=mesh,
        in_specs=(P(("grp", "own"), None), P(("grp", "own")), P("own", None), P("own", None)),
        out_specs=(P("own", None), P("own", "grp")),
        check_vma=False,
    )
```

```python
import functools

import jax
import jax.numpy as jnp
from jax import lax
from jax.experimental import pallas as pl
from jax.experimental.pallas import tpu as pltpu
from jax.sharding import PartitionSpec as P

KC_OWN = 8
CAP = 8
LANES = 128


def torus(owners):
    fast = 1
    while fast * fast < owners:
        fast *= 2
    return owners // fast, fast


def turned(a, b, r):
    return ((a, b), (-b, a), (-a, -b), (b, -a))[r]


def far_first(nx, ny):
    if (nx, ny) != (8, 8):
        return [(i % nx, i // nx) for i in range(nx * ny)]
    order = []
    for g in range(16):
        a, b = 4 - g // 4, 3 - g % 4
        if (a, b) == (4, 0):
            order += [(4, 0), (0, 4), (0, 0), (4, 4)]
        else:
            order += [turned(a, b, r) for r in range(4)]
    return [(a % nx, b % ny) for a, b in order]


def iota(shape, dim):
    return lax.broadcasted_iota(jnp.int32, shape, dim)


def to_column(row):
    n = row.shape[1]
    return jnp.sum(jnp.where(iota((n, n), 0) == iota((n, n), 1), row, 0.0), axis=1, keepdims=True)


def kernel(
    owners, groups,
    emb_hbm, cid_hbm, count_hbm, fine_hbm,
    fine_new, coarse_new,
    emb, cid, fine_count, fine,
    out_rows, in_rows, out_tags, in_tags, rows, resp, own_part, sib_out, sib_in,
    out4, in4, out3, in3, out2, in2, out1, in1, cnt_out, cnt_in, num_out, num_in, table, ring_new,
    load, send_rows, recv_rows, send_tags, recv_tags, send_sib, recv_sib,
    send_sum, recv_sum, send_cnt, recv_cnt, send_num, recv_num, send_ring, recv_ring, send_gs, recv_gs, keep,
):
    nx, ny = torus(owners)
    nz = groups // 2
    rows_dev, width = emb.shape
    half = width // 2
    f_own = fine.shape[0]
    f_half = f_own // 2
    f_quarter = f_own // 4
    chunk = min(16, owners)
    chunks = owners // chunk
    slots = chunk * CAP
    bf16, f32 = jnp.bfloat16, jnp.float32

    own = lax.axis_index("own")
    grp = lax.axis_index("grp")
    mx, my = own // ny, own % ny
    z, core = grp // 2, grp % 2
    sibling = {"grp": z * 2 + 1 - core}

    order = far_first(nx, ny)
    here = order.index((0, 0))

    def peer(kx, ky):
        return {"own": lax.rem(mx + kx + nx, nx) * ny + lax.rem(my + ky + ny, ny)}

    def for_peers(lo, hi, act):
        if (nx, ny) != (8, 8):
            for i in range(lo, hi):
                if i != here:
                    act(i, peer(*order[i]))
            return

        def four(g):
            a, b = 4 - g // 4, 3 - lax.rem(g, 4)
            for r in range(4):
                act(g * 4 + r, peer(*turned(a, b, r)))

        first, last = lo // 4, hi // 4
        if first <= 3 < last:
            pl.loop(first, 3)(four)
            for i in (12, 13, 15):
                act(i, peer(*order[i]))
            first = 4
        pl.loop(first, last)(four)

    def along(k):
        return lax.rem(z + k + nz, nz)

    def at_z(k):
        return {"grp": along(k) * 2 + core}

    def mate(i):
        return {"grp": lax.rem(grp + i, groups)}

    def remote(src, dst, send, recv, device):
        return pltpu.make_async_remote_copy(
            src_ref=src, dst_ref=dst, send_sem=send, recv_sem=recv,
            device_id=device, device_id_type=pl.DeviceIdType.MESH,
        )

    def take(ref, sem):
        pltpu.make_async_copy(ref, ref, sem).wait()

    loads = [
        pltpu.make_async_copy(src, dst, load.at[n])
        for n, (src, dst) in enumerate(
            ((cid_hbm, cid), (emb_hbm, emb), (count_hbm, fine_count), (fine_hbm, fine))
        )
    ]
    for copy in loads:
        copy.start()

    barrier = pltpu.get_barrier_semaphore()

    def greet(i, device):
        pl.semaphore_signal(barrier, inc=1, device_id=device, device_id_type=pl.DeviceIdType.MESH)

    for_peers(0, owners, greet)

    @pl.loop(1, groups)
    def _(i):
        greet(i, mate(i))

    loads[0].wait()
    ids = cid[...]
    owner = lax.shift_right_logical(ids, 3)
    kx = (lax.shift_right_logical(owner, ny.bit_length() - 1) - mx) & (nx - 1)
    ky = ((owner & (ny - 1)) - my) & (ny - 1)
    away = kx * ny + ky
    block = jnp.zeros_like(away)
    for i, (a, b) in enumerate(order):
        block = jnp.where(away == a * ny + b, i, block)
    owner_row = owner.astype(f32)
    owner_col = to_column(owner_row)
    local_col = to_column((ids & (KC_OWN - 1)).astype(f32))
    square = (rows_dev, rows_dev)
    same = owner_col == owner_row
    place_row = jnp.sum(jnp.where(same & (iota(square, 0) < iota(square, 1)), 1.0, 0.0), axis=0, keepdims=True)
    place_col = jnp.sum(jnp.where(same & (iota(square, 1) < iota(square, 0)), 1.0, 0.0), axis=1, keepdims=True)
    target = block * (2 * CAP) + place_row.astype(jnp.int32)

    pick = (iota((owners, rows_dev), 0) == block).astype(bf16)
    lane = (iota((rows_dev, LANES), 1) & (CAP - 1)).astype(f32)
    spread = jnp.where(place_col == lane, local_col + 1.0, 0.0).astype(bf16)
    tags = jnp.dot(pick, spread, preferred_element_type=f32)
    out_tags[...] = tags.reshape(owners, 1, LANES)
    in_tags[here] = out_tags[here]

    loads[1].wait()
    @pl.loop(0, chunks)
    def _(c):
        tall = 2 * CAP * chunk
        at = iota((tall, rows_dev), 0) + c * tall
        low = (at == target).astype(bf16)
        high = (at == target + CAP).astype(bf16)
        made = jnp.dot(low, emb[:, :half], preferred_element_type=f32)
        made += jnp.dot(high, emb[:, half:], preferred_element_type=f32)
        out_rows[pl.ds(c * chunk, chunk)] = made.astype(bf16).reshape(chunk, 2 * CAP, half)

    pl.semaphore_wait(barrier, owners + groups - 2)
    for c in range(chunks):

        def send(i, device):
            remote(out_tags.at[i], in_tags.at[i], send_tags.at[0], recv_tags.at[c], device).start()
            remote(out_rows.at[i], in_rows.at[i], send_rows.at[0], recv_rows.at[c], device).start()

        for_peers(c * chunk, (c + 1) * chunk, send)

    in_rows[here] = out_rows[here]

    loads[2].wait()
    loads[3].wait()
    fine_rows = fine[...].astype(f32)
    squares = jnp.sum(fine_rows * fine_rows, axis=1, keepdims=True)
    index_col, index_row = iota((f_own, 1), 0), iota((1, f_own), 1)
    cluster_col = jnp.zeros((f_own, 1), f32)
    cluster_row = jnp.zeros((1, f_own), f32)
    start = jnp.zeros((1, 1), jnp.int32)
    for k in range(KC_OWN - 1):
        start = start + fine_count[:, k:k + 1]
        cluster_col += (index_col >= start).astype(f32)
        cluster_row += (index_row >= start).astype(f32)
    table[...] = jnp.broadcast_to(squares * 0.5, table.shape)
    member_of = (cluster_row == iota((KC_OWN, f_own), 0).astype(f32)).astype(f32)

    @pl.loop(0, chunks)
    def _(c):
        def come(count):
            if count > 0:
                take(in_tags.at[pl.ds(c * chunk, count)], recv_tags.at[c])
                take(in_rows.at[pl.ds(c * chunk, count)], recv_rows.at[c])

        pl.when(c == here // chunk)(functools.partial(come, chunk - 1))
        pl.when(c != here // chunk)(functools.partial(come, chunk))
        these = pl.ds(c * chunk, chunk)
        tag = in_tags[these].reshape(chunk, LANES)[:, :slots]
        tag = jnp.where(iota((chunk, slots), 1) // CAP == iota((chunk, slots), 0), tag, 0.0)
        label = jnp.sum(tag, axis=0, keepdims=True) - 1.0
        wide = in_rows[these].astype(f32).reshape(chunk, 2, CAP, half)
        low = wide[:, 0].reshape(slots, half).astype(bf16)
        high = wide[:, 1].reshape(slots, half).astype(bf16)
        at = pl.ds(pl.multiple_of(c * slots, slots), slots)
        for b in range(nz // 2):
            rows[b, at, :] = low[:, b * LANES:(b + 1) * LANES]
            rows[nz // 2 + b, at, :] = high[:, b * LANES:(b + 1) * LANES]
        flip = (((1,), (1,)), ((), ()))
        dots = lax.dot_general(fine[:, :half], low, flip, preferred_element_type=f32)
        dots += lax.dot_general(fine[:, half:], high, flip, preferred_element_type=f32)
        member = cluster_col == label
        scores = (dots - table[:, :slots]) * (width ** -0.5)
        masked = jnp.where(member, scores, -1e30)
        top = jnp.max(masked, axis=0, keepdims=True)
        weights = jnp.where(member, jnp.exp(masked - top), 0.0)
        total = jnp.sum(weights, axis=0, keepdims=True)
        empty = (label < 0.0).astype(f32)
        resp[:, at] = (weights / (total + empty)).astype(bf16)

    mine, other = pl.ds(core * f_half, f_half), pl.ds((1 - core) * f_half, f_half)

    def weigh(off):
        b = along(off)
        sib_out[b] = jnp.dot(resp[other, :], rows[b], preferred_element_type=f32).astype(bf16)
        remote(sib_out.at[b], sib_in.at[b], send_sib.at[b], recv_sib.at[b], sibling).start()
        own_part[b] = jnp.dot(resp[mine, :], rows[b], preferred_element_type=f32)

    def count_up():
        ones = jnp.ones((8, resp.shape[1]), bf16)
        counts = lax.dot_general(ones, resp[...], (((1,), (1,)), ((), ())), preferred_element_type=f32)
        cnt_out[...] = counts[0:1, :]
        cnt_in[0] = counts[0:1, :]

        @pl.loop(1, groups)
        def _(i):
            remote(cnt_out, cnt_in.at[i], send_cnt.at[0], recv_cnt.at[0], mate(i)).start()

    def chip(off, q):
        piece = pl.ds(q * f_quarter, f_quarter)
        b = along(off)
        return own_part[b, piece, :] + sib_in[b, piece, :].astype(f32)

    def both(off):
        b = along(off)
        take(sib_in.at[b], recv_sib.at[b])
        return own_part[b] + sib_in[b].astype(f32)

    sent = []

    def give(n, src, dst, k):
        remote(src, dst, send_sum.at[n], recv_sum.at[n], at_z(k)).start()
        sent.append((src, send_sum.at[n]))

    def got(n, ref):
        take(ref, recv_sum.at[n])
        return ref[...].astype(f32)

    @pl.loop(0, 3)
    def _(n):
        weigh(jnp.where(n == 0, 4, jnp.where(n == 1, 3, -3)))

    total = both(4).astype(bf16)
    for q, k in ((0, -2), (1, 2)):
        out4[q] = total[q * f_quarter:(q + 1) * f_quarter]
        give(q, out4.at[q], in4.at[q], k)
    for n, off, k in ((0, -3, -1), (1, 3, 1)):
        out3[n] = both(off).astype(bf16)
        give(2 + n, out3.at[n], in3.at[n], k)
    @pl.loop(0, 4)
    def _(n):
        weigh((2 - n // 2) * (1 - 2 * lax.rem(n, 2)))

    count_up()
    for n, off in ((0, -1), (1, 1)):
        out1[n] = both(off).astype(bf16)
        give(4 + n, out1.at[n], in1.at[n], off)
    weigh(0)
    for off in (-2, 2, 0):
        take(sib_in.at[along(off)], recv_sib.at[along(off)])
    for n, off in ((0, -2), (1, 2)):
        take(in3.at[n], recv_sum.at[2 + n])
    for q in range(2):
        for n, off in ((1, 2), (0, -2)) if q == 0 else ((0, -2), (1, 2)):
            total = chip(off, q) + in3[n, pl.ds(q * f_quarter, f_quarter), :].astype(f32)
            if n == q:
                total += got(q, in4.at[q])
            out2[n, q] = total.astype(bf16)
            give(6 + 2 * n + q, out2.at[n, q], in2.at[n, q], off)

    take(cnt_in.at[pl.ds(1, groups - 1)], recv_cnt.at[0])
    weight = jnp.sum(cnt_in[...], axis=0) + 1.0
    weight_col = to_column(jnp.where(core == 0, weight[:, :f_half], weight[:, f_half:]))

    ring = []

    def part_of(off, q):
        return ring_new.at[along(off), pl.ds(q * f_quarter, f_quarter), :]

    def spread_to(n, off, q, k):
        piece = part_of(off, q)
        remote(piece, piece, send_ring.at[n], recv_ring.at[n], at_z(k)).start()
        ring.append((piece, send_ring.at[n]))

    def arrived(n, off, q):
        take(part_of(off, q), recv_ring.at[n])

    def hand_over(off):
        b = along(off)
        place = fine_new.at[mine, pl.ds(pl.multiple_of(b * LANES, LANES), LANES)]
        remote(ring_new.at[b], place, send_gs.at[0], recv_gs.at[0], sibling).start()
        pltpu.make_async_copy(ring_new.at[b], place, keep.at[0]).start()

    columns = pl.ds(pl.multiple_of(z * LANES, LANES), LANES)
    numers = []
    for n in range(2):
        take(in1.at[n], recv_sum.at[4 + n])
    for q in range(2):
        piece = pl.ds(q * f_quarter, f_quarter)
        old = fine[pl.ds(pl.multiple_of(core * f_half + q * f_quarter, f_quarter), f_quarter), columns]
        numer = chip(0, q) + old.astype(f32)
        numer += in1[0, piece, :].astype(f32) + in1[1, piece, :].astype(f32)
        numer += got(6 + q, in2.at[0, q]) + got(8 + q, in2.at[1, q])
        numers.append(numer)
        ring_new[z, piece, :] = (numer / weight_col[q * f_quarter:(q + 1) * f_quarter]).astype(bf16)
        spread_to(q, 0, q, 2)
        spread_to(2 + q, 0, q, -2)
    for q in range(2):
        spread_to(4 + q, 0, q, 1)
        spread_to(6 + q, 0, q, -1)
    hand_over(0)

    member_half = jnp.where(core == 0, member_of[:, :f_half], member_of[:, f_half:])
    num = sum(
        lax.dot_general(
            member_half[:, q * f_quarter:(q + 1) * f_quarter], numers[q], (((1,), (0,)), ((), ())),
            preferred_element_type=f32, precision=lax.Precision.HIGHEST,
        )
        for q in range(2)
    )
    num_out[...] = num
    remote(num_out, num_in, send_num.at[0], recv_num.at[0], sibling).start()
    den = jnp.sum(member_of * weight, axis=1, keepdims=True)

    arrived(0, -2, 0)
    spread_to(12, -2, 0, 2)
    spread_to(8, -2, 0, 1)
    arrived(2, 2, 0)
    spread_to(10, 2, 0, -1)
    arrived(3, 2, 1)
    spread_to(13, 2, 1, -2)
    spread_to(11, 2, 1, -1)
    arrived(1, -2, 1)
    spread_to(9, -2, 1, 1)
    hand_over(-2)
    hand_over(2)
    for n, off in ((4, -1), (6, 1)):
        arrived(n, off, 0)
        arrived(n + 1, off, 1)
        hand_over(off)

    take(num_in, recv_num.at[0])
    coarse = (num + num_in[...]) / den
    coarse = jnp.where(core == 0, coarse[:, :LANES // 2], coarse[:, LANES // 2:])
    coarse_new[...] = coarse.astype(bf16)

    if owners > 1:
        take(out_rows.at[pl.ds(1, owners - 1)], send_rows.at[0])
        take(out_tags.at[pl.ds(1, owners - 1)], send_tags.at[0])
    take(cnt_in.at[pl.ds(1, groups - 1)], send_cnt.at[0])
    take(num_out, send_num.at[0])
    for b in range(nz):
        take(sib_out.at[b], send_sib.at[b])
    for ref, sem in sent:
        take(ref, sem)

    for n, off in ((8, -3), (10, 3), (12, 4)):
        arrived(n, off, 0)
        arrived(n + 1, off, 1)
        hand_over(off)

    for ref, sem in ring:
        take(ref, sem)
    take(ring_new, send_gs.at[0])
    take(ring_new, keep.at[0])
    take(fine_new.at[other, :], recv_gs.at[0])


def per_device(owners, groups, embeddings, coarse_id, fine_count, fine):
    rows_dev, width = embeddings.shape
    f_own = fine.shape[0]
    nz = groups // 2
    assert nz == 8
    chunks = max(1, owners // 16)
    slots = owners * CAP
    bf16, f32 = jnp.bfloat16, jnp.float32
    vmem, dma = pltpu.VMEM, pltpu.SemaphoreType.DMA
    anywhere = pl.BlockSpec(memory_space=pl.ANY)
    tile = (f_own // 2, LANES)
    piece = (f_own // 4, LANES)
    return pl.pallas_call(
        functools.partial(kernel, owners, groups),
        out_shape=(
            jax.ShapeDtypeStruct((f_own, width), bf16),
            jax.ShapeDtypeStruct((KC_OWN, width // groups), bf16),
        ),
        in_specs=[anywhere] * 4,
        out_specs=(anywhere, pl.BlockSpec(memory_space=pltpu.VMEM)),
        scratch_shapes=[
            vmem((rows_dev, width), bf16),
            vmem((1, rows_dev), jnp.int32),
            vmem((1, KC_OWN), jnp.int32),
            vmem((f_own, width), bf16),
            vmem((owners, 2 * CAP, width // 2), bf16),
            vmem((owners, 2 * CAP, width // 2), bf16),
            vmem((owners, 1, LANES), f32),
            vmem((owners, 1, LANES), f32),
            vmem((nz, slots, LANES), bf16),
            vmem((f_own, slots), bf16),
            vmem((nz,) + tile, f32),
            vmem((nz,) + tile, bf16),
            vmem((nz,) + tile, bf16),
            vmem((2,) + piece, bf16),
            vmem((2,) + piece, bf16),
            vmem((2,) + tile, bf16),
            vmem((2,) + tile, bf16),
            vmem((2, 2) + piece, bf16),
            vmem((2, 2) + piece, bf16),
            vmem((2,) + tile, bf16),
            vmem((2,) + tile, bf16),
            vmem((1, f_own), f32),
            vmem((groups, 1, f_own), f32),
            vmem((KC_OWN, LANES), f32),
            vmem((KC_OWN, LANES), f32),
            vmem((f_own, LANES), f32),
            vmem((nz,) + tile, bf16),
            dma((4,)),
            dma((1,)), dma((chunks,)), dma((1,)), dma((chunks,)), dma((nz,)), dma((nz,)),
            dma((10,)), dma((10,)), dma((1,)), dma((1,)), dma((1,)), dma((1,)),
            dma((14,)), dma((14,)), dma((1,)), dma((1,)), dma((1,)),
        ],
        compiler_params=pltpu.CompilerParams(
            collective_id=0, has_side_effects=True, vmem_limit_bytes=56 * 1024 * 1024
        ),
    )(embeddings, coarse_id.reshape(1, rows_dev), fine_count, fine)


def solution(mesh):
    return jax.shard_map(
        functools.partial(per_device, mesh.shape["own"], mesh.shape["grp"]),
        mesh=mesh,
        in_specs=(P(("grp", "own"), None), P(("grp", "own")), P("own", None), P("own", None)),
        out_specs=(P("own", None), P("own", "grp")),
        check_vma=False,
    )
```

```python
import functools

import jax
import jax.numpy as jnp
from jax import lax
from jax.experimental import pallas as pl
from jax.experimental.pallas import tpu as pltpu
from jax.sharding import PartitionSpec as P

KC_OWN = 8
CAP = 8
LANES = 128


def torus(owners):
    fast = 1
    while fast * fast < owners:
        fast *= 2
    return owners // fast, fast


def turned(a, b, r):
    return ((a, b), (-b, a), (-a, -b), (b, -a))[r]


def far_first(nx, ny):
    if (nx, ny) != (8, 8):
        return [(i % nx, i // nx) for i in range(nx * ny)]
    order = []
    for g in range(16):
        a, b = 4 - g // 4, 3 - g % 4
        if (a, b) == (4, 0):
            order += [(4, 0), (0, 4), (0, 0), (4, 4)]
        else:
            order += [turned(a, b, r) for r in range(4)]
    return [(a % nx, b % ny) for a, b in order]


def iota(shape, dim):
    return lax.broadcasted_iota(jnp.int32, shape, dim)


def to_column(row):
    n = row.shape[1]
    return jnp.sum(jnp.where(iota((n, n), 0) == iota((n, n), 1), row, 0.0), axis=1, keepdims=True)


def kernel(
    owners, groups,
    emb_hbm, cid_hbm, count_hbm, fine_hbm,
    fine_new, coarse_new,
    emb, cid, fine_count, fine,
    out_rows, in_rows, out_tags, in_tags, rows, resp, own_part, sib_out, sib_in,
    out4, in4, out3, in3, out2, in2, out1, in1, cnt_out, cnt_in, num_out, num_in, table, ring_new,
    load, send_rows, recv_rows, send_tags, recv_tags, send_sib, recv_sib,
    send_sum, recv_sum, send_cnt, recv_cnt, send_num, recv_num, send_ring, recv_ring, send_gs, recv_gs, keep,
):
    nx, ny = torus(owners)
    nz = groups // 2
    rows_dev, width = emb.shape
    half = width // 2
    f_own = fine.shape[0]
    f_half = f_own // 2
    f_quarter = f_own // 4
    chunk = min(16, owners)
    chunks = owners // chunk
    slots = chunk * CAP
    bf16, f32 = jnp.bfloat16, jnp.float32

    own = lax.axis_index("own")
    grp = lax.axis_index("grp")
    mx, my = own // ny, own % ny
    z, core = grp // 2, grp % 2
    sibling = {"grp": z * 2 + 1 - core}

    order = far_first(nx, ny)
    here = order.index((0, 0))

    def peer(kx, ky):
        return {"own": lax.rem(mx + kx + nx, nx) * ny + lax.rem(my + ky + ny, ny)}

    def for_peers(lo, hi, act):
        if (nx, ny) != (8, 8):
            for i in range(lo, hi):
                if i != here:
                    act(i, peer(*order[i]))
            return

        def four(g):
            a, b = 4 - g // 4, 3 - lax.rem(g, 4)
            for r in range(4):
                act(g * 4 + r, peer(*turned(a, b, r)))

        first, last = lo // 4, hi // 4
        if first <= 3 < last:
            pl.loop(first, 3)(four)
            for i in (12, 13, 15):
                act(i, peer(*order[i]))
            first = 4
        pl.loop(first, last)(four)

    def along(k):
        return lax.rem(z + k + nz, nz)

    def at_z(k):
        return {"grp": along(k) * 2 + core}

    def mate(i):
        return {"grp": lax.rem(grp + i, groups)}

    def remote(src, dst, send, recv, device):
        return pltpu.make_async_remote_copy(
            src_ref=src, dst_ref=dst, send_sem=send, recv_sem=recv,
            device_id=device, device_id_type=pl.DeviceIdType.MESH,
        )

    def take(ref, sem):
        pltpu.make_async_copy(ref, ref, sem).wait()

    loads = [
        pltpu.make_async_copy(src, dst, load.at[n])
        for n, (src, dst) in enumerate(
            ((cid_hbm, cid), (emb_hbm, emb), (count_hbm, fine_count), (fine_hbm, fine))
        )
    ]
    for copy in loads:
        copy.start()

    barrier = pltpu.get_barrier_semaphore()

    def greet(i, device):
        pl.semaphore_signal(barrier, inc=1, device_id=device, device_id_type=pl.DeviceIdType.MESH)

    for_peers(0, owners, greet)

    @pl.loop(1, groups)
    def _(i):
        greet(i, mate(i))

    loads[0].wait()
    ids = cid[...]
    owner = lax.shift_right_logical(ids, 3)
    kx = (lax.shift_right_logical(owner, ny.bit_length() - 1) - mx) & (nx - 1)
    ky = ((owner & (ny - 1)) - my) & (ny - 1)
    away = kx * ny + ky
    block = jnp.zeros_like(away)
    for i, (a, b) in enumerate(order):
        block = jnp.where(away == a * ny + b, i, block)
    owner_row = owner.astype(f32)
    owner_col = to_column(owner_row)
    local_col = to_column((ids & (KC_OWN - 1)).astype(f32))
    square = (rows_dev, rows_dev)
    same = owner_col == owner_row
    place_row = jnp.sum(jnp.where(same & (iota(square, 0) < iota(square, 1)), 1.0, 0.0), axis=0, keepdims=True)
    place_col = jnp.sum(jnp.where(same & (iota(square, 1) < iota(square, 0)), 1.0, 0.0), axis=1, keepdims=True)
    target = block * (2 * CAP) + place_row.astype(jnp.int32)

    pick = (iota((owners, rows_dev), 0) == block).astype(bf16)
    lane = (iota((rows_dev, LANES), 1) & (CAP - 1)).astype(f32)
    spread = jnp.where(place_col == lane, local_col + 1.0, 0.0).astype(bf16)
    tags = jnp.dot(pick, spread, preferred_element_type=f32)
    out_tags[...] = tags.reshape(owners, 1, LANES)
    in_tags[here] = out_tags[here]

    loads[1].wait()
    @pl.loop(0, chunks)
    def _(c):
        tall = 2 * CAP * chunk
        at = iota((tall, rows_dev), 0) + c * tall
        low = (at == target).astype(bf16)
        high = (at == target + CAP).astype(bf16)
        made = jnp.dot(low, emb[:, :half], preferred_element_type=f32)
        made += jnp.dot(high, emb[:, half:], preferred_element_type=f32)
        out_rows[pl.ds(c * chunk, chunk)] = made.astype(bf16).reshape(chunk, 2 * CAP, half)

    pl.semaphore_wait(barrier, owners + groups - 2)
    for c in range(chunks):

        def send(i, device):
            remote(out_tags.at[i], in_tags.at[i], send_tags.at[0], recv_tags.at[c], device).start()
            remote(out_rows.at[i], in_rows.at[i], send_rows.at[0], recv_rows.at[c], device).start()

        for_peers(c * chunk, (c + 1) * chunk, send)

    in_rows[here] = out_rows[here]

    loads[2].wait()
    loads[3].wait()
    fine_rows = fine[...].astype(f32)
    squares = jnp.sum(fine_rows * fine_rows, axis=1, keepdims=True)
    index_col, index_row = iota((f_own, 1), 0), iota((1, f_own), 1)
    cluster_col = jnp.zeros((f_own, 1), f32)
    cluster_row = jnp.zeros((1, f_own), f32)
    start = jnp.zeros((1, 1), jnp.int32)
    for k in range(KC_OWN - 1):
        start = start + fine_count[:, k:k + 1]
        cluster_col += (index_col >= start).astype(f32)
        cluster_row += (index_row >= start).astype(f32)
    table[...] = jnp.broadcast_to(squares * 0.5, table.shape)
    member_of = (cluster_row == iota((KC_OWN, f_own), 0).astype(f32)).astype(f32)

    @pl.loop(0, chunks)
    def _(c):
        def come(count):
            if count > 0:
                take(in_tags.at[pl.ds(c * chunk, count)], recv_tags.at[c])
                take(in_rows.at[pl.ds(c * chunk, count)], recv_rows.at[c])

        pl.when(c == here // chunk)(functools.partial(come, chunk - 1))
        pl.when(c != here // chunk)(functools.partial(come, chunk))
        these = pl.ds(c * chunk, chunk)
        tag = in_tags[these].reshape(chunk, LANES)[:, :slots]
        tag = jnp.where(iota((chunk, slots), 1) // CAP == iota((chunk, slots), 0), tag, 0.0)
        label = jnp.sum(tag, axis=0, keepdims=True) - 1.0
        wide = in_rows[these].astype(f32).reshape(chunk, 2, CAP, half)
        low = wide[:, 0].reshape(slots, half).astype(bf16)
        high = wide[:, 1].reshape(slots, half).astype(bf16)
        at = pl.ds(pl.multiple_of(c * slots, slots), slots)
        for b in range(nz // 2):
            rows[b, at, :] = low[:, b * LANES:(b + 1) * LANES]
            rows[nz // 2 + b, at, :] = high[:, b * LANES:(b + 1) * LANES]
        flip = (((1,), (1,)), ((), ()))
        dots = lax.dot_general(fine[:, :half], low, flip, preferred_element_type=f32)
        dots += lax.dot_general(fine[:, half:], high, flip, preferred_element_type=f32)
        member = cluster_col == label
        scores = (dots - table[:, :slots]) * (width ** -0.5)
        masked = jnp.where(member, scores, -1e30)
        top = jnp.max(masked, axis=0, keepdims=True)
        weights = jnp.where(member, jnp.exp(masked - top), 0.0)
        total = jnp.sum(weights, axis=0, keepdims=True)
        empty = (label < 0.0).astype(f32)
        resp[:, at] = (weights / (total + empty)).astype(bf16)

    mine, other = pl.ds(core * f_half, f_half), pl.ds((1 - core) * f_half, f_half)

    def weigh(off):
        b = along(off)
        sib_out[b] = jnp.dot(resp[other, :], rows[b], preferred_element_type=f32).astype(bf16)
        remote(sib_out.at[b], sib_in.at[b], send_sib.at[b], recv_sib.at[b], sibling).start()
        own_part[b] = jnp.dot(resp[mine, :], rows[b], preferred_element_type=f32)

    def count_up():
        ones = jnp.ones((8, resp.shape[1]), bf16)
        counts = lax.dot_general(ones, resp[...], (((1,), (1,)), ((), ())), preferred_element_type=f32)
        cnt_out[...] = counts[0:1, :]
        cnt_in[0] = counts[0:1, :]

        @pl.loop(1, groups)
        def _(i):
            remote(cnt_out, cnt_in.at[i], send_cnt.at[0], recv_cnt.at[0], mate(i)).start()

    def chip(off, q):
        piece = pl.ds(q * f_quarter, f_quarter)
        b = along(off)
        return own_part[b, piece, :] + sib_in[b, piece, :].astype(f32)

    def both(off):
        b = along(off)
        take(sib_in.at[b], recv_sib.at[b])
        return own_part[b] + sib_in[b].astype(f32)

    sent = []

    def give(n, src, dst, k):
        remote(src, dst, send_sum.at[n], recv_sum.at[n], at_z(k)).start()
        sent.append((src, send_sum.at[n]))

    def got(n, ref):
        take(ref, recv_sum.at[n])
        return ref[...].astype(f32)

    @pl.loop(0, 3)
    def _(n):
        weigh(jnp.where(n == 0, 4, jnp.where(n == 1, 3, -3)))

    total = both(4).astype(bf16)
    for q, k in ((0, -2), (1, 2)):
        out4[q] = total[q * f_quarter:(q + 1) * f_quarter]
        give(q, out4.at[q], in4.at[q], k)
    for n, off in ((0, -3), (1, 3)):
        out3[n] = both(off).astype(bf16)
    for q in range(2):
        piece = pl.ds(q * f_quarter, f_quarter)
        for n, k in ((1, 1), (0, -1)):
            give(2 + n + 8 * q, out3.at[n, piece, :], in3.at[n, piece, :], k)
    @pl.loop(0, 4)
    def _(n):
        weigh((2 - n // 2) * (1 - 2 * lax.rem(n, 2)))

    count_up()
    for n, off in ((0, -1), (1, 1)):
        out1[n] = both(off).astype(bf16)
        give(4 + n, out1.at[n], in1.at[n], off)
    weigh(0)
    for off in (-2, 2, 0):
        take(sib_in.at[along(off)], recv_sib.at[along(off)])
    for q in range(2):
        piece = pl.ds(q * f_quarter, f_quarter)
        for n, off in ((1, 2), (0, -2)) if q == 0 else ((0, -2), (1, 2)):
            total = chip(off, q) + got(2 + n + 8 * q, in3.at[n, piece, :])
            if n == q:
                total += got(q, in4.at[q])
            out2[n, q] = total.astype(bf16)
            give(6 + 2 * n + q, out2.at[n, q], in2.at[n, q], off)

    take(cnt_in.at[pl.ds(1, groups - 1)], recv_cnt.at[0])
    weight = jnp.sum(cnt_in[...], axis=0) + 1.0
    weight_col = to_column(jnp.where(core == 0, weight[:, :f_half], weight[:, f_half:]))

    ring = []

    def part_of(off, q):
        return ring_new.at[along(off), pl.ds(q * f_quarter, f_quarter), :]

    def spread_to(n, off, q, k):
        piece = part_of(off, q)
        remote(piece, piece, send_ring.at[n], recv_ring.at[n], at_z(k)).start()
        ring.append((piece, send_ring.at[n]))

    def arrived(n, off, q):
        take(part_of(off, q), recv_ring.at[n])

    def hand_over(off):
        b = along(off)
        place = fine_new.at[mine, pl.ds(pl.multiple_of(b * LANES, LANES), LANES)]
        remote(ring_new.at[b], place, send_gs.at[0], recv_gs.at[0], sibling).start()
        pltpu.make_async_copy(ring_new.at[b], place, keep.at[0]).start()

    columns = pl.ds(pl.multiple_of(z * LANES, LANES), LANES)
    numers = []
    for n in range(2):
        take(in1.at[n], recv_sum.at[4 + n])
    for q in range(2):
        piece = pl.ds(q * f_quarter, f_quarter)
        old = fine[pl.ds(pl.multiple_of(core * f_half + q * f_quarter, f_quarter), f_quarter), columns]
        numer = chip(0, q) + old.astype(f32)
        numer += in1[0, piece, :].astype(f32) + in1[1, piece, :].astype(f32)
        numer += got(6 + q, in2.at[0, q]) + got(8 + q, in2.at[1, q])
        numers.append(numer)
        ring_new[z, piece, :] = (numer / weight_col[q * f_quarter:(q + 1) * f_quarter]).astype(bf16)
        spread_to(q, 0, q, 2)
        spread_to(2 + q, 0, q, -2)
    for q in range(2):
        spread_to(4 + q, 0, q, 1)
        spread_to(6 + q, 0, q, -1)
    hand_over(0)

    member_half = jnp.where(core == 0, member_of[:, :f_half], member_of[:, f_half:])
    num = sum(
        lax.dot_general(
            member_half[:, q * f_quarter:(q + 1) * f_quarter], numers[q], (((1,), (0,)), ((), ())),
            preferred_element_type=f32, precision=lax.Precision.HIGHEST,
        )
        for q in range(2)
    )
    num_out[...] = num
    remote(num_out, num_in, send_num.at[0], recv_num.at[0], sibling).start()
    den = jnp.sum(member_of * weight, axis=1, keepdims=True)

    arrived(0, -2, 0)
    spread_to(12, -2, 0, 2)
    spread_to(8, -2, 0, 1)
    arrived(2, 2, 0)
    spread_to(10, 2, 0, -1)
    arrived(3, 2, 1)
    spread_to(13, 2, 1, -2)
    spread_to(11, 2, 1, -1)
    arrived(1, -2, 1)
    spread_to(9, -2, 1, 1)
    hand_over(-2)
    hand_over(2)
    for n, off in ((4, -1), (6, 1)):
        arrived(n, off, 0)
        arrived(n + 1, off, 1)
        hand_over(off)

    take(num_in, recv_num.at[0])
    coarse = (num + num_in[...]) / den
    coarse = jnp.where(core == 0, coarse[:, :LANES // 2], coarse[:, LANES // 2:])
    coarse_new[...] = coarse.astype(bf16)

    if owners > 1:
        take(out_rows.at[pl.ds(1, owners - 1)], send_rows.at[0])
        take(out_tags.at[pl.ds(1, owners - 1)], send_tags.at[0])
    take(cnt_in.at[pl.ds(1, groups - 1)], send_cnt.at[0])
    take(num_out, send_num.at[0])
    for b in range(nz):
        take(sib_out.at[b], send_sib.at[b])
    for ref, sem in sent:
        take(ref, sem)

    for n, off in ((8, -3), (10, 3), (12, 4)):
        arrived(n, off, 0)
        arrived(n + 1, off, 1)
        hand_over(off)

    for ref, sem in ring:
        take(ref, sem)
    take(ring_new, send_gs.at[0])
    take(ring_new, keep.at[0])
    take(fine_new.at[other, :], recv_gs.at[0])


def per_device(owners, groups, embeddings, coarse_id, fine_count, fine):
    rows_dev, width = embeddings.shape
    f_own = fine.shape[0]
    nz = groups // 2
    assert nz == 8
    chunks = max(1, owners // 16)
    slots = owners * CAP
    bf16, f32 = jnp.bfloat16, jnp.float32
    vmem, dma = pltpu.VMEM, pltpu.SemaphoreType.DMA
    anywhere = pl.BlockSpec(memory_space=pl.ANY)
    tile = (f_own // 2, LANES)
    piece = (f_own // 4, LANES)
    return pl.pallas_call(
        functools.partial(kernel, owners, groups),
        out_shape=(
            jax.ShapeDtypeStruct((f_own, width), bf16),
            jax.ShapeDtypeStruct((KC_OWN, width // groups), bf16),
        ),
        in_specs=[anywhere] * 4,
        out_specs=(anywhere, pl.BlockSpec(memory_space=pltpu.VMEM)),
        scratch_shapes=[
            vmem((rows_dev, width), bf16),
            vmem((1, rows_dev), jnp.int32),
            vmem((1, KC_OWN), jnp.int32),
            vmem((f_own, width), bf16),
            vmem((owners, 2 * CAP, width // 2), bf16),
            vmem((owners, 2 * CAP, width // 2), bf16),
            vmem((owners, 1, LANES), f32),
            vmem((owners, 1, LANES), f32),
            vmem((nz, slots, LANES), bf16),
            vmem((f_own, slots), bf16),
            vmem((nz,) + tile, f32),
            vmem((nz,) + tile, bf16),
            vmem((nz,) + tile, bf16),
            vmem((2,) + piece, bf16),
            vmem((2,) + piece, bf16),
            vmem((2,) + tile, bf16),
            vmem((2,) + tile, bf16),
            vmem((2, 2) + piece, bf16),
            vmem((2, 2) + piece, bf16),
            vmem((2,) + tile, bf16),
            vmem((2,) + tile, bf16),
            vmem((1, f_own), f32),
            vmem((groups, 1, f_own), f32),
            vmem((KC_OWN, LANES), f32),
            vmem((KC_OWN, LANES), f32),
            vmem((f_own, LANES), f32),
            vmem((nz,) + tile, bf16),
            dma((4,)),
            dma((1,)), dma((chunks,)), dma((1,)), dma((chunks,)), dma((nz,)), dma((nz,)),
            dma((12,)), dma((12,)), dma((1,)), dma((1,)), dma((1,)), dma((1,)),
            dma((14,)), dma((14,)), dma((1,)), dma((1,)), dma((1,)),
        ],
        compiler_params=pltpu.CompilerParams(
            collective_id=0, has_side_effects=True, vmem_limit_bytes=56 * 1024 * 1024
        ),
    )(embeddings, coarse_id.reshape(1, rows_dev), fine_count, fine)


def solution(mesh):
    return jax.shard_map(
        functools.partial(per_device, mesh.shape["own"], mesh.shape["grp"]),
        mesh=mesh,
        in_specs=(P(("grp", "own"), None), P(("grp", "own")), P("own", None), P("own", None)),
        out_specs=(P("own", None), P("own", "grp")),
        check_vma=False,
    )
```
